512 devices in a mesh: wide: 32 (over x_lo, z), row: 4 (over y), col: 4 (over x_hi, core).
Axes of the slice: x: 4 (x_hi: 2, x_lo: 2; x = x_hi * 2 + x_lo), y: 4, z: 16, core: 2. Of those that a mesh axis runs over, the one named last changes fastest.
Arguments:
- tokens: bfloat16 [256, 12288], P('wide', ('row', 'col')), may hold values from -6 to 6
- in_weight: bfloat16 [12288, 24576], P(('row', 'col'), 'wide'), may hold values from -0.0546875 to 0.0546875
- out_weight: bfloat16 [24576, 12288], P('wide', ('row', 'col')), may hold values from -0.0390625 to 0.0390625
- out_grad: bfloat16 [256, 12288], P('wide', ('row', 'col')), may hold values from -1.5 to 1.5
Outputs:
- output: bfloat16 [256, 12288], P('wide', ('row', 'col'))
- tokens_grad: bfloat16 [256, 12288], P('wide', ('row', 'col'))
- in_weight_grad: bfloat16 [12288, 24576], P(('row', 'col'), 'wide')
- out_weight_grad: bfloat16 [24576, 12288], P('wide', ('row', 'col'))
The draws below stay inside these ranges and needn't reach their ends.
All inputs are finite; a program needn't handle non-finite values.
Results may differ from the reference program's by a relative error of at most 0.005.
Values may be sent and summed in bfloat16 or wider, within the bound.
No kernel may reach another device: no remote copies, remote signals or barrier semaphores. Data moves between devices by JAX's collectives and lax.ppermute only.
A program may use at most 64 MiB of HBM per device.

```python
import jax
import jax.numpy as jnp

D = 12288
FF = 24576
TOKENS = 256


def level_of(rng, shape, pieces, smallest, largest):
    level = 1.0
    for dim, blocks in pieces:
        steps = jax.random.uniform(jax.random.fold_in(jax.random.fold_in(rng, 6), dim), (blocks,), jnp.float32, smallest / len(pieces), largest / len(pieces))
        level = level * jnp.repeat(jnp.exp(steps), shape[dim] // blocks).reshape((-1,) + (1,) * (len(shape) - 1 - dim))
    return level


def noise(key, shape, width, most, split=(), dtype=jnp.bfloat16):
    result = width * jax.random.normal(key, shape, jnp.float32)
    if split:
        result = result * level_of(key, shape, split, -0.22, 0.18)
    return jnp.clip(result, -most, most).astype(dtype)


def setup_inputs(seed: int = 0) -> dict:
    key_of = jax.random.split(jax.random.key(seed), 5)
    tokens = noise(key_of[0], (TOKENS, D), 1.0, 6.0, ((0, 32), (1, 16)))
    in_weight = noise(key_of[1], (D, FF), D ** -0.5, 0.0546875, ((0, 16), (1, 32)))
    out_weight = noise(key_of[2], (FF, D), FF ** -0.5, 0.0390625, ((0, 32), (1, 16)))
    out_grad = noise(key_of[3], (TOKENS, D), (TOKENS ** -0.25), 1.5, ((0, 32), (1, 16)))
    return dict(tokens=tokens, in_weight=in_weight, out_weight=out_weight, out_grad=out_grad)


def gelu_value(preact):
    inner_term = 0.7978845608028654 * (preact + 0.044715 * preact * preact * preact)
    return 0.5 * preact * (1.0 + jnp.tanh(inner_term))


def gelu_slope(preact):
    tangent = jnp.tanh(0.7978845608028654 * (preact + 0.044715 * preact * preact * preact))
    return 0.5 * (1.0 + tangent) + 0.5 * preact * (1.0 - tangent * tangent) * 0.7978845608028654 * (1.0 + 3.0 * 0.044715 * preact * preact)


def reference(tokens, in_weight, out_weight, out_grad):
    hidden_pre = jnp.dot(tokens, in_weight, preferred_element_type=jnp.float32)
    active = gelu_value(hidden_pre).astype(jnp.bfloat16)
    output = jnp.dot(active, out_weight, preferred_element_type=jnp.float32).astype(jnp.bfloat16)
    grad_active = jnp.dot(out_grad, out_weight.T, preferred_element_type=jnp.float32)
    grad_pre = (grad_active * gelu_slope(hidden_pre)).astype(jnp.bfloat16)
    out_weight_grad = jnp.dot(active.T, out_grad, preferred_element_type=jnp.float32).astype(jnp.bfloat16)
    in_weight_grad = jnp.dot(tokens.T, grad_pre, preferred_element_type=jnp.float32).astype(jnp.bfloat16)
    tokens_grad = jnp.dot(grad_pre, in_weight.T, preferred_element_type=jnp.float32).astype(jnp.bfloat16)
    return output, tokens_grad, in_weight_grad, out_weight_grad
```

```python
import jax
import jax.numpy as jnp
from jax import lax
from jax.sharding import Mesh
from jax.sharding import PartitionSpec as P

HIDDEN = ("y", "x_hi", "core")
C = 0.7978845608028654


def gelu_both(v):
    t = jnp.tanh(C * (v + 0.044715 * v * v * v))
    value = 0.5 * v * (1.0 + t)
    slope = 0.5 * (1.0 + t) + 0.5 * v * (1.0 - t * t) * C * (1.0 + 3.0 * 0.044715 * v * v)
    return value, slope


def dot(left, right, dims):
    return lax.dot_general(left, right, (dims, ((), ())), preferred_element_type=jnp.float32)


def per_device(tokens, in_weight, out_weight, out_grad):
    width = tokens.shape[1]
    parts = lax.axis_size(HIDDEN)
    both = jnp.concatenate([tokens, out_grad], axis=1)
    both = lax.all_gather(both, "x_lo", axis=0, tiled=True)
    both = lax.all_gather(both, "z", axis=0, tiled=True)
    all_tokens, all_grads = both[:, :width], both[:, width:]
    rows = both.shape[0]

    pre_part = dot(all_tokens, in_weight, ((1,), (0,))).astype(jnp.bfloat16)
    grad_part = dot(all_grads, out_weight, ((1,), (1,))).astype(jnp.bfloat16)
    sums = jnp.concatenate([pre_part, grad_part], axis=1).reshape(parts, rows // parts, -1)
    sums = lax.all_to_all(sums, HIDDEN, 0, 0, tiled=True)
    sums = jnp.sum(sums.astype(jnp.float32), axis=0)
    hidden = in_weight.shape[1]
    value, slope = gelu_both(sums[:, :hidden])
    share = jnp.concatenate([value, sums[:, hidden:] * slope], axis=1).astype(jnp.bfloat16)
    share = jnp.broadcast_to(share[None], (parts,) + share.shape)
    share = lax.all_to_all(share, HIDDEN, 0, 0, tiled=True).reshape(rows, -1)
    active, grad_pre = share[:, :hidden], share[:, hidden:]

    out_part = dot(active, out_weight, ((1,), (0,))).astype(jnp.bfloat16)
    back_part = dot(grad_pre, in_weight, ((1,), (1,))).astype(jnp.bfloat16)
    ends = jnp.concatenate([out_part, back_part], axis=1)
    group = lax.axis_size(("z", "x_lo"))
    ends = ends.reshape(group, rows // group, -1)
    ends = lax.all_to_all(ends, ("z", "x_lo"), 0, 0, tiled=True)
    out_weight_grad = dot(active, all_grads, ((0,), (0,))).astype(jnp.bfloat16)
    in_weight_grad = dot(all_tokens, grad_pre, ((0,), (0,))).astype(jnp.bfloat16)
    ends = jnp.sum(ends.astype(jnp.float32), axis=0).astype(jnp.bfloat16)
    return ends[:, :width], ends[:, width:], in_weight_grad, out_weight_grad


def solution(mesh):
    fine = Mesh(mesh.devices.reshape(2, -1, mesh.shape["row"], 2, 2), ("x_lo", "z", "y", "x_hi", "core"))
    wide = ("x_lo", "z")
    specs = (P(wide, HIDDEN), P(HIDDEN, wide), P(wide, HIDDEN), P(wide, HIDDEN))
    outs = (P(wide, HIDDEN), P(wide, HIDDEN), P(HIDDEN, wide), P(wide, HIDDEN))
    return jax.shard_map(per_device, mesh=fine, in_specs=specs, out_specs=outs, check_vma=False)
```

```python
import jax
import jax.numpy as jnp
from jax import lax
from jax.sharding import Mesh
from jax.sharding import PartitionSpec as P

HIDDEN = ("y", "x_hi", "core")
NEAR = ("z_lo", "x_lo")
FAR = ("z_hi",)
C = 0.7978845608028654


def gelu_both(v):
    t = jnp.tanh(C * (v + 0.044715 * v * v * v))
    value = 0.5 * v * (1.0 + t)
    slope = 0.5 * (1.0 + t) + 0.5 * v * (1.0 - t * t) * C * (1.0 + 3.0 * 0.044715 * v * v)
    return value, slope


def dot(left, right, dims):
    return lax.dot_general(left, right, (dims, ((), ())), preferred_element_type=jnp.float32)


def gather(rows, axes):
    copies = jnp.broadcast_to(rows[None], (lax.axis_size(axes),) + rows.shape)
    return lax.all_to_all(copies, axes, 0, 0, tiled=True).reshape(-1, rows.shape[1])


def spread_sum(part, axes):
    blocks = part.reshape(lax.axis_size(axes), -1, part.shape[1])
    return jnp.sum(lax.all_to_all(blocks, axes, 0, 0, tiled=True).astype(jnp.float32), axis=0)


def per_device(tokens, in_weight, out_weight, out_grad):
    width = tokens.shape[1]
    both = jnp.concatenate([tokens, out_grad], axis=1)
    both = gather(gather(both, FAR), NEAR)
    all_tokens, all_grads = both[:, :width], both[:, width:]

    pre_part = dot(all_tokens, in_weight, ((1,), (0,))).astype(jnp.bfloat16)
    grad_part = dot(all_grads, out_weight, ((1,), (1,))).astype(jnp.bfloat16)
    sums = spread_sum(jnp.concatenate([pre_part, grad_part], axis=1), HIDDEN)
    hidden = in_weight.shape[1]
    value, slope = gelu_both(sums[:, :hidden])
    share = jnp.concatenate([value, sums[:, hidden:] * slope], axis=1).astype(jnp.bfloat16)
    share = gather(share, HIDDEN)
    active, grad_pre = share[:, :hidden], share[:, hidden:]

    out_part = dot(active, out_weight, ((1,), (0,))).astype(jnp.bfloat16)
    back_part = dot(grad_pre, in_weight, ((1,), (1,))).astype(jnp.bfloat16)
    ends = spread_sum(jnp.concatenate([out_part, back_part], axis=1), NEAR)
    out_weight_grad = dot(active, all_grads, ((0,), (0,))).astype(jnp.bfloat16)
    in_weight_grad = dot(all_tokens, grad_pre, ((0,), (0,))).astype(jnp.bfloat16)
    ends = spread_sum(ends, FAR).astype(jnp.bfloat16)
    return ends[:, :width], ends[:, width:], in_weight_grad, out_weight_grad


def solution(mesh):
    fine = Mesh(mesh.devices.reshape(2, -1, 4, mesh.shape["row"], 2, 2), ("x_lo", "z_hi", "z_lo", "y", "x_hi", "core"))
    wide = ("x_lo", "z_hi", "z_lo")
    specs = (P(wide, HIDDEN), P(HIDDEN, wide), P(wide, HIDDEN), P(wide, HIDDEN))
    outs = (P(wide, HIDDEN), P(wide, HIDDEN), P(HIDDEN, wide), P(wide, HIDDEN))
    return jax.shard_map(per_device, mesh=fine, in_specs=specs, out_specs=outs, check_vma=False)
```

```python
import jax
import jax.numpy as jnp
from jax import lax
from jax.sharding import Mesh
from jax.sharding import PartitionSpec as P

HIDDEN = ("y", "x_hi", "core")
ORDER = ("core", "y", "x_hi")
NEAR = ("x_lo", "z_near")
FAR = ("z_far",)
C = 0.7978845608028654


def gelu_both(v):
    t = jnp.tanh(C * (v + 0.044715 * v * v * v))
    value = 0.5 * v * (1.0 + t)
    slope = 0.5 * (1.0 + t) + 0.5 * v * (1.0 - t * t) * C * (1.0 + 3.0 * 0.044715 * v * v)
    return value, slope


def dot(left, right, dims):
    return lax.dot_general(left, right, (dims, ((), ())), preferred_element_type=jnp.float32)


def gather(rows, axes):
    copies = jnp.broadcast_to(rows[None], (lax.axis_size(axes),) + rows.shape)
    return lax.all_to_all(copies, axes, 0, 0, tiled=True).reshape(-1, rows.shape[1])


def spread_sum(part, axes):
    blocks = part.reshape(lax.axis_size(axes), -1, part.shape[1])
    return jnp.sum(lax.all_to_all(blocks, axes, 0, 0, tiled=True).astype(jnp.float32), axis=0)


def per_device(tokens, in_weight, out_weight, out_grad):
    width = tokens.shape[1]
    both = jnp.concatenate([tokens, out_grad], axis=1)
    both = gather(gather(both, FAR), NEAR)
    all_tokens, all_grads = both[:, :width], both[:, width:]

    pre_part = dot(all_tokens, in_weight, ((1,), (0,))).astype(jnp.bfloat16)
    grad_part = dot(all_grads, out_weight, ((1,), (1,))).astype(jnp.bfloat16)
    sums = spread_sum(jnp.concatenate([pre_part, grad_part], axis=1), ORDER)
    hidden = in_weight.shape[1]
    value, slope = gelu_both(sums[:, :hidden])
    share = jnp.concatenate([value, sums[:, hidden:] * slope], axis=1).astype(jnp.bfloat16)
    share = lax.all_gather(gather(share, ORDER[1:]), ORDER[0], axis=0, tiled=True)
    active, grad_pre = share[:, :hidden], share[:, hidden:]

    out_part = dot(active, out_weight, ((1,), (0,))).astype(jnp.bfloat16)
    back_part = dot(grad_pre, in_weight, ((1,), (1,))).astype(jnp.bfloat16)
    ends = spread_sum(jnp.concatenate([out_part, back_part], axis=1), NEAR).astype(jnp.bfloat16)
    out_weight_grad = dot(active, all_grads, ((0,), (0,))).astype(jnp.bfloat16)
    in_weight_grad = dot(all_tokens, grad_pre, ((0,), (0,))).astype(jnp.bfloat16)
    ends = spread_sum(ends, FAR).astype(jnp.bfloat16)
    return ends[:, :width], ends[:, width:], in_weight_grad, out_weight_grad


def solution(mesh):
    fine = Mesh(mesh.devices.reshape(2, -1, 2, mesh.shape["row"], 2, 2), ("x_lo", "z_far", "z_near", "y", "x_hi", "core"))
    wide = ("x_lo", "z_far", "z_near")
    specs = (P(wide, HIDDEN), P(HIDDEN, wide), P(wide, HIDDEN), P(wide, HIDDEN))
    outs = (P(wide, HIDDEN), P(wide, HIDDEN), P(HIDDEN, wide), P(wide, HIDDEN))
    return jax.shard_map(per_device, mesh=fine, in_specs=specs, out_specs=outs, check_vma=False)
```

```python
import jax
import jax.numpy as jnp
from jax import lax
from jax.sharding import Mesh
from jax.sharding import PartitionSpec as P

HIDDEN = ("y", "x_hi", "core")
CHIPS = ("y", "x_hi")
NEAR = ("x_lo", "z_near")
FAR = ("z_far",)
C = 0.7978845608028654


def gelu_both(v):
    t = jnp.tanh(C * (v + 0.044715 * v * v * v))
    value = 0.5 * v * (1.0 + t)
    slope = 0.5 * (1.0 + t) + 0.5 * v * (1.0 - t * t) * C * (1.0 + 3.0 * 0.044715 * v * v)
    return value, slope


def dot(left, right, dims):
    return lax.dot_general(left, right, (dims, ((), ())), preferred_element_type=jnp.float32)


def partner(rows, axes, k):
    return lax.ppermute(rows, axes, [(i, i ^ k) for i in range(lax.axis_size(axes))])


def gather(rows, axes):
    copies = jnp.broadcast_to(rows[None], (lax.axis_size(axes),) + rows.shape)
    return lax.all_to_all(copies, axes, 0, 0, tiled=True).reshape(-1, rows.shape[1])


def spread_sum(part, axes):
    blocks = part.reshape(lax.axis_size(axes), -1, part.shape[1])
    return jnp.sum(lax.all_to_all(blocks, axes, 0, 0, tiled=True).astype(jnp.float32), axis=0)


def gather_near(rows):
    others = [partner(rows, NEAR, k) for k in range(1, lax.axis_size(NEAR))]
    return jnp.concatenate([rows] + others, axis=0)


def sum_near(part):
    blocks = jnp.split(part, lax.axis_size(NEAR), axis=0)
    total = blocks[0].astype(jnp.float32)
    for other in [partner(block, NEAR, k) for k, block in enumerate(blocks) if k]:
        total = total + other.astype(jnp.float32)
    return total


def per_device(tokens, in_weight, out_weight, out_grad):
    width, hidden = in_weight.shape
    both = jnp.concatenate([tokens, out_grad], axis=1)
    both = gather_near(gather(both, FAR))
    all_tokens, all_grads = both[:, :width], both[:, width:]

    def hidden_part(half):
        rows = both.shape[0] // 2
        here = lax.dynamic_slice_in_dim(both, half * rows, rows, 0)
        pre_part = dot(here[:, :width], in_weight, ((1,), (0,)))
        grad_part = dot(here[:, width:], out_weight, ((1,), (1,)))
        return jnp.concatenate([pre_part, grad_part], axis=1)

    core = lax.axis_index("core")
    other = partner(hidden_part(1 - core), "core", 1)
    sums = spread_sum((hidden_part(core) + other).astype(jnp.bfloat16), CHIPS)
    value, slope = gelu_both(sums[:, :hidden])
    share = jnp.concatenate([value, sums[:, hidden:] * slope], axis=1).astype(jnp.bfloat16)
    share = lax.all_gather(gather(share, CHIPS), "core", axis=0, tiled=True)
    active, grad_pre = share[:, :hidden], share[:, hidden:]

    out_part = dot(active, out_weight, ((1,), (0,))).astype(jnp.bfloat16)
    back_part = dot(grad_pre, in_weight, ((1,), (1,))).astype(jnp.bfloat16)
    ends = sum_near(jnp.concatenate([out_part, back_part], axis=1)).astype(jnp.bfloat16)
    out_weight_grad = dot(active, all_grads, ((0,), (0,))).astype(jnp.bfloat16)
    in_weight_grad = dot(all_tokens, grad_pre, ((0,), (0,))).astype(jnp.bfloat16)
    ends = spread_sum(ends, FAR).astype(jnp.bfloat16)
    return ends[:, :width], ends[:, width:], in_weight_grad, out_weight_grad


def solution(mesh):
    fine = Mesh(mesh.devices.reshape(2, -1, 2, mesh.shape["row"], 2, 2), ("x_lo", "z_far", "z_near", "y", "x_hi", "core"))
    wide = ("x_lo", "z_far", "z_near")
    specs = (P(wide, HIDDEN), P(HIDDEN, wide), P(wide, HIDDEN), P(wide, HIDDEN))
    outs = (P(wide, HIDDEN), P(wide, HIDDEN), P(HIDDEN, wide), P(wide, HIDDEN))
    return jax.shard_map(per_device, mesh=fine, in_specs=specs, out_specs=outs, check_vma=False)
```

```python
import jax
import jax.numpy as jnp
from jax import lax
from jax.sharding import Mesh
from jax.sharding import PartitionSpec as P

HIDDEN = ("y", "x_hi", "core")
ORDER = ("core", "y", "x_hi")
NEAR = ("x_lo", "z_near")
FAR = ("z_far",)
C = 0.7978845608028654


def gelu_both(v):
    t = jnp.tanh(C * (v + 0.044715 * v * v * v))
    value = 0.5 * v * (1.0 + t)
    slope = 0.5 * (1.0 + t) + 0.5 * v * (1.0 - t * t) * C * (1.0 + 3.0 * 0.044715 * v * v)
    return value, slope


def dot(left, right, dims):
    return lax.dot_general(left, right, (dims, ((), ())), preferred_element_type=jnp.float32)


def gather(rows, axes):
    copies = jnp.broadcast_to(rows[None], (lax.axis_size(axes),) + rows.shape)
    return lax.all_to_all(copies, axes, 0, 0, tiled=True).reshape(-1, rows.shape[1])


def spread_sum(part, axes):
    blocks = part.reshape(lax.axis_size(axes), -1, part.shape[1])
    return jnp.sum(lax.all_to_all(blocks, axes, 0, 0, tiled=True).astype(jnp.float32), axis=0)


def per_device(tokens, in_weight, out_weight, out_grad):
    width = tokens.shape[1]
    first, tokens = lax.optimization_barrier((lax.axis_index("core") == 0, tokens))
    both = jnp.concatenate([tokens, out_grad], axis=1)
    both = gather(gather(both, FAR), NEAR)
    all_tokens, all_grads = both[:, :width], both[:, width:]

    half = all_tokens.shape[0] // 2
    pre_part = dot(all_tokens, in_weight, ((1,), (0,)))
    grad_part = dot(all_grads, out_weight, ((1,), (1,)))
    low = jnp.concatenate([pre_part[:half], grad_part[:half]], axis=1)
    high = jnp.concatenate([pre_part[half:], grad_part[half:]], axis=1)
    other = lax.all_gather(jnp.where(first, high, low).astype(jnp.bfloat16), "core", axis=0, tiled=True)
    other = jnp.where(first, other[half:], other[:half]).astype(jnp.float32)
    sums = spread_sum((jnp.where(first, low, high) + other).astype(jnp.bfloat16), ORDER[1:])
    hidden = in_weight.shape[1]
    value, slope = gelu_both(sums[:, :hidden])
    share = jnp.concatenate([value, sums[:, hidden:] * slope], axis=1).astype(jnp.bfloat16)
    share = lax.all_gather(gather(share, ORDER[1:]), ORDER[0], axis=0, tiled=True)
    active, grad_pre = share[:, :hidden], share[:, hidden:]

    out_part = dot(active, out_weight, ((1,), (0,))).astype(jnp.bfloat16)
    back_part = dot(grad_pre, in_weight, ((1,), (1,))).astype(jnp.bfloat16)
    ends = spread_sum(jnp.concatenate([out_part, back_part], axis=1), NEAR).astype(jnp.bfloat16)
    out_weight_grad = dot(active, all_grads, ((0,), (0,))).astype(jnp.bfloat16)
    in_weight_grad = dot(all_tokens, grad_pre, ((0,), (0,))).astype(jnp.bfloat16)
    ends = spread_sum(ends, FAR).astype(jnp.bfloat16)
    return ends[:, :width], ends[:, width:], in_weight_grad, out_weight_grad


def solution(mesh):
    fine = Mesh(mesh.devices.reshape(2, -1, 2, mesh.shape["row"], 2, 2), ("x_lo", "z_far", "z_near", "y", "x_hi", "core"))
    wide = ("x_lo", "z_far", "z_near")
    specs = (P(wide, HIDDEN), P(HIDDEN, wide), P(wide, HIDDEN), P(wide, HIDDEN))
    outs = (P(wide, HIDDEN), P(wide, HIDDEN), P(HIDDEN, wide), P(wide, HIDDEN))
    return jax.shard_map(per_device, mesh=fine, in_specs=specs, out_specs=outs, check_vma=False)
```

```python
import jax
import jax.numpy as jnp
from jax import lax
from jax.sharding import Mesh
from jax.sharding import PartitionSpec as P

HIDDEN = ("y", "x_hi", "core")
ORDER = ("core", "y", "x_hi")
NEAR = ("x_lo", "z_near")
FAR = ("z2", "z4", "z8")
C = 0.7978845608028654


def gelu_both(v):
    t = jnp.tanh(C * (v + 0.044715 * v * v * v))
    value = 0.5 * v * (1.0 + t)
    slope = 0.5 * (1.0 + t) + 0.5 * v * (1.0 - t * t) * C * (1.0 + 3.0 * 0.044715 * v * v)
    return value, slope


def dot(left, right, dims):
    return lax.dot_general(left, right, (dims, ((), ())), preferred_element_type=jnp.float32)


def gather(rows, axes):
    copies = jnp.broadcast_to(rows[None], (lax.axis_size(axes),) + rows.shape)
    return lax.all_to_all(copies, axes, 0, 0, tiled=True).reshape(-1, rows.shape[1])


def spread_sum(part, axes):
    blocks = part.reshape(lax.axis_size(axes), -1, part.shape[1])
    return jnp.sum(lax.all_to_all(blocks, axes, 0, 0, tiled=True).astype(jnp.float32), axis=0)


def per_device(tokens, in_weight, out_weight, out_grad):
    width = tokens.shape[1]
    first, tokens = lax.optimization_barrier((lax.axis_index("core") == 0, tokens))
    both = jnp.concatenate([tokens, out_grad], axis=1)
    both = gather(gather(both, FAR), NEAR)
    all_tokens, all_grads = both[:, :width], both[:, width:]

    half = all_tokens.shape[0] // 2
    pre_part = dot(all_tokens, in_weight, ((1,), (0,)))
    grad_part = dot(all_grads, out_weight, ((1,), (1,)))
    low = jnp.concatenate([pre_part[:half], grad_part[:half]], axis=1)
    high = jnp.concatenate([pre_part[half:], grad_part[half:]], axis=1)
    other = lax.all_gather(jnp.where(first, high, low).astype(jnp.bfloat16), "core", axis=0, tiled=True)
    other = jnp.where(first, other[half:], other[:half]).astype(jnp.float32)
    sums = spread_sum((jnp.where(first, low, high) + other).astype(jnp.bfloat16), ORDER[1:])
    hidden = in_weight.shape[1]
    value, slope = gelu_both(sums[:, :hidden])
    share = jnp.concatenate([value, sums[:, hidden:] * slope], axis=1).astype(jnp.bfloat16)
    share = lax.all_gather(gather(share, ORDER[1:]), ORDER[0], axis=0, tiled=True)
    active, grad_pre = share[:, :hidden], share[:, hidden:]

    out_part = dot(active, out_weight, ((1,), (0,))).astype(jnp.bfloat16)
    back_part = dot(grad_pre, in_weight, ((1,), (1,))).astype(jnp.bfloat16)
    ends = spread_sum(jnp.concatenate([out_part, back_part], axis=1), NEAR).astype(jnp.bfloat16)
    out_weight_grad = dot(active, all_grads, ((0,), (0,))).astype(jnp.bfloat16)
    in_weight_grad = dot(all_tokens, grad_pre, ((0,), (0,))).astype(jnp.bfloat16)
    ends = spread_sum(ends, FAR).astype(jnp.bfloat16)
    return ends[:, :width], ends[:, width:], in_weight_grad, out_weight_grad


def solution(mesh):
    fine = Mesh(mesh.devices.reshape(2, 2, 2, 2, 2, mesh.shape["row"], 2, 2), ("x_lo", "z8", "z4", "z2", "z_near", "y", "x_hi", "core"))
    wide = ("x_lo", "z8", "z4", "z2", "z_near")
    specs = (P(wide, HIDDEN), P(HIDDEN, wide), P(wide, HIDDEN), P(wide, HIDDEN))
    outs = (P(wide, HIDDEN), P(wide, HIDDEN), P(HIDDEN, wide), P(wide, HIDDEN))
    return jax.shard_map(per_device, mesh=fine, in_specs=specs, out_specs=outs, check_vma=False)
```

```python
import jax
import jax.numpy as jnp
from jax import lax
from jax.sharding import Mesh
from jax.sharding import PartitionSpec as P

HIDDEN = ("y", "x_hi", "core")
ORDER = ("core", "y", "x_hi")
NEAR = ("x_lo", "z_near")
FAR = ("z2", "z4", "z8")
C = 0.7978845608028654


def gelu_both(v):
    t = jnp.tanh(C * (v + 0.044715 * v * v * v))
    value = 0.5 * v * (1.0 + t)
    slope = 0.5 * (1.0 + t) + 0.5 * v * (1.0 - t * t) * C * (1.0 + 3.0 * 0.044715 * v * v)
    return value, slope


def dot(left, right, dims):
    return lax.dot_general(left, right, (dims, ((), ())), preferred_element_type=jnp.float32)


def gather(rows, axes):
    copies = jnp.broadcast_to(rows[None], (lax.axis_size(axes),) + rows.shape)
    return lax.all_to_all(copies, axes, 0, 0, tiled=True).reshape(-1, rows.shape[1])


def spread_sum(part, axes):
    blocks = part.reshape(lax.axis_size(axes), -1, part.shape[1])
    return jnp.sum(lax.all_to_all(blocks, axes, 0, 0, tiled=True).astype(jnp.float32), axis=0)


def per_device(tokens, in_weight, out_weight, out_grad):
    width = tokens.shape[1]
    both = jnp.concatenate([tokens, out_grad], axis=1)
    both = gather(gather(both, FAR), NEAR)
    all_tokens, all_grads = both[:, :width], both[:, width:]

    pre_part = dot(all_tokens, in_weight, ((1,), (0,))).astype(jnp.bfloat16)
    grad_part = dot(all_grads, out_weight, ((1,), (1,))).astype(jnp.bfloat16)
    sums = spread_sum(jnp.concatenate([pre_part, grad_part], axis=1), ORDER)
    hidden = in_weight.shape[1]
    value, slope = gelu_both(sums[:, :hidden])
    share = jnp.concatenate([value, sums[:, hidden:] * slope], axis=1).astype(jnp.bfloat16)
    share = lax.all_gather(gather(share, ORDER[1:]), ORDER[0], axis=0, tiled=True)
    active, grad_pre = share[:, :hidden], share[:, hidden:]

    out_part = dot(active, out_weight, ((1,), (0,))).astype(jnp.bfloat16)
    back_part = dot(grad_pre, in_weight, ((1,), (1,))).astype(jnp.bfloat16)
    ends = spread_sum(jnp.concatenate([out_part, back_part], axis=1), NEAR).astype(jnp.bfloat16)
    out_weight_grad = dot(active, all_grads, ((0,), (0,))).astype(jnp.bfloat16)
    in_weight_grad = dot(all_tokens, grad_pre, ((0,), (0,))).astype(jnp.bfloat16)
    ends = spread_sum(ends, FAR).astype(jnp.bfloat16)
    return ends[:, :width], ends[:, width:], in_weight_grad, out_weight_grad


def solution(mesh):
    fine = Mesh(mesh.devices.reshape(2, 2, 2, 2, 2, mesh.shape["row"], 2, 2), ("x_lo", "z8", "z4", "z2", "z_near", "y", "x_hi", "core"))
    wide = ("x_lo", "z8", "z4", "z2", "z_near")
    specs = (P(wide, HIDDEN), P(HIDDEN, wide), P(wide, HIDDEN), P(wide, HIDDEN))
    outs = (P(wide, HIDDEN), P(wide, HIDDEN), P(HIDDEN, wide), P(wide, HIDDEN))
    return jax.shard_map(per_device, mesh=fine, in_specs=specs, out_specs=outs, check_vma=False)
```
